512 devices in a mesh: outer: 16 (over z, core), inner: 32 (over x, y).
Axes of the slice: x: 4, y: 8, z: 8, core: 2. Of those that a mesh axis runs over, the one named last changes fastest.
Arguments:
- queries: bfloat16 [65536, 1024], P(('outer', 'inner')), may hold values from -16 to 16
- keys: bfloat16 [65536, 128], P(('outer', 'inner')), may hold values from -8 to 8
- values: bfloat16 [65536, 128], P(('outer', 'inner')), may hold values from -6 to 6
- d_out: bfloat16 [65536, 1024], P(('outer', 'inner')), may hold values from -6 to 6
- doc_ids: int32 [65536], replicated, may hold values from 0 to 63, never falling along the last dimension, each value on 1 to 2048 neighbouring positions
Outputs:
- attended: bfloat16 [65536, 1024], P(('outer', 'inner'))
- grad_queries: bfloat16 [65536, 1024], P(('outer', 'inner'))
- grad_keys: bfloat16 [65536, 128], P(('outer', 'inner'))
- grad_values: bfloat16 [65536, 128], P(('outer', 'inner'))
The draws below stay inside these ranges and needn't reach their ends.
Inputs may be any that keep to these rules, and one draw needn't show every extreme that they name: `doc_ids`: never falls along the sequence; each document holds 1 to 2048 tokens, one exactly 2048.
All inputs are finite; a program needn't handle non-finite values.
Results may differ from the reference program's by a relative error of at most 0.012.
The reference program's roundings to bfloat16 on the way (of `probs_low` and `score_grad`) count: a program that leaves them out, or rounds other values in their place, can miss the bound.
Values may be sent and summed in bfloat16 or wider, within the bound.
No kernel may reach another device: no remote copies, remote signals or barrier semaphores. Data moves between devices by JAX's collectives and lax.ppermute only.
A program may use at most 64 MiB of HBM per device.

```python
import math
import jax
import jax.numpy as jnp
import numpy as np
from jax import lax

HD = 128
HQ = 8
TOK_DEV = 128
WINDOW = 1024
SEQ = 65536
DOCS = 64
DOC_MOST = 2048


def draw_queries(key, part):
    own_key = jax.random.fold_in(key, 11)
    full = jnp.clip(3.0 * jax.random.normal(own_key, (SEQ, HQ, HD), jnp.float32), -14.0, 14.0)
    return full.reshape(SEQ, HQ * HD).astype(jnp.bfloat16)


def draw_keys(key, part):
    own_key = jax.random.fold_in(key, 13)
    full = jnp.clip(jax.random.normal(own_key, (SEQ, HD), jnp.float32), -6.0, 6.0)
    return full.astype(jnp.bfloat16)


def shard_levels(stream_key, shape, shards, low, high):
    def one(position, shards_of):
        steps = jax.random.uniform(jax.random.fold_in(jax.random.fold_in(stream_key, 6), position), (shards_of,), jnp.float32, low / len(shards), high / len(shards))
        return jnp.repeat(jnp.exp(steps), shape[position] // shards_of).reshape((-1,) + (1,) * (len(shape) - position - 1))

    gain = one(*shards[0])
    for cut in shards[1:]:
        gain = gain * one(*cut)
    return gain


def profile(count, total, reach, slope):
    portions = [(1 << 20) // math.isqrt(grade ** slope) + 1 for grade in range(2, count + 1)]
    surplus, given = total - reach - (count - 1), [1] * (count - 1)
    while surplus > 0:
        free = [i for i in range(count - 1) if given[i] < reach]
        pool, left = sum([portions[i] for i in free]), surplus
        for i in free:
            more = min(reach - given[i], max(1, left * portions[i] // pool), surplus)
            given[i] = given[i] + more
            surplus = surplus - more
    return np.array([reach] + given)


def uneven(rng, count, total, limit, slope):
    if count == 2:
        one = jax.random.randint(rng, (), max(1, total - limit), min(limit, total - 1) + 1)
        return jnp.stack([one, total - one])
    lengths = jnp.asarray(profile(count, total, limit, slope), jnp.int32)
    pairs = (count - 1) // 2
    source_of, sink = lengths[1:1 + 2 * pairs:2], lengths[2:2 + 2 * pairs:2]
    margin = jnp.minimum(source_of - 1, limit - sink)
    moved = jax.random.randint(jax.random.fold_in(rng, 1), (pairs,), 0, 1 << 20) % (margin + 1)
    lengths = lengths.at[1:1 + 2 * pairs:2].set(source_of - moved).at[2:2 + 2 * pairs:2].set(sink + moved)
    return lengths[jax.random.permutation(jax.random.fold_in(rng, 2), count)]


def scatter_about(rng, shape, scale, bound, cuts=(), held_as=jnp.bfloat16):
    result = jax.random.normal(rng, shape, jnp.float32) * scale
    if len(cuts) > 0:
        result = shard_levels(rng, shape, cuts, -0.22, 0.18) * result
    return jnp.clip(result, min=-bound, max=bound).astype(held_as)


def setup_inputs(seed: int = 0) -> dict:
    arg_keys = jax.random.split(jax.random.key(seed), 6)
    queries = draw_queries(jax.random.fold_in(arg_keys[5], 71), 0)
    keys = draw_keys(jax.random.fold_in(arg_keys[5], 71), 0)
    values = scatter_about(arg_keys[2], (SEQ, HD), 1.0, 6.0, ((0, 512),))
    d_out = scatter_about(arg_keys[3], (SEQ, HQ * HD), 1.0, 6.0, ((0, 512),))
    doc_ids = jnp.searchsorted(jnp.cumsum(uneven(arg_keys[4], DOCS, SEQ, DOC_MOST, 1)), jnp.arange(SEQ), side="right").astype(jnp.int32)
    return {"queries": queries, "keys": keys, "values": values, "d_out": d_out, "doc_ids": doc_ids}


def reference(queries, keys, values, d_out, doc_ids):
    score_scale = 1.0 / math.sqrt(HD)
    blocks = SEQ // TOK_DEV
    lead = WINDOW - TOK_DEV
    key_pad = jnp.concatenate([jnp.zeros((lead, HD), jnp.bfloat16), keys], axis=0)
    value_pad = jnp.concatenate([jnp.zeros((lead, HD), jnp.bfloat16), values], axis=0)
    doc_pad = jnp.concatenate([jnp.full((lead,), -1, jnp.int32), doc_ids.astype(jnp.int32)], axis=0)
    query_blocks = queries.reshape(blocks, TOK_DEV * HQ, HD)
    grad_blocks = d_out.reshape(blocks, TOK_DEV * HQ, HD)
    inside = jnp.arange(TOK_DEV, dtype=jnp.int32)
    spread = jnp.arange(WINDOW, dtype=jnp.int32)
    block_ids = jnp.arange(blocks, dtype=jnp.int32)

    def one_block(grad_all, block_in):
        block, query_rows, grad_rows = block_in
        start = (block * TOK_DEV).astype(jnp.int32)
        key_blk = lax.dynamic_slice_in_dim(key_pad, start, WINDOW)
        value_blk = lax.dynamic_slice_in_dim(value_pad, start, WINDOW)
        doc_blk = lax.dynamic_slice_in_dim(doc_pad, start, WINDOW)
        key_pos = start - lead + spread
        query_doc = lax.dynamic_slice_in_dim(doc_ids.astype(jnp.int32), start, TOK_DEV)
        row_pos = jnp.repeat(start + inside, HQ)
        row_doc = jnp.repeat(query_doc, HQ)
        visible = (key_pos[None, :] <= row_pos[:, None]) & (key_pos[None, :] >= 0) & (doc_blk[None, :] == row_doc[:, None])
        raw_scores = jnp.dot(query_rows, key_blk.T, preferred_element_type=jnp.float32) * score_scale
        scores = jnp.where(visible, raw_scores, -jnp.inf)
        row_top = lax.optimization_barrier(jnp.max(scores, axis=1))
        weights = jnp.exp(scores - row_top[:, None])
        row_total = lax.optimization_barrier(jnp.sum(weights, axis=1))
        row_accum = jnp.dot(weights, value_blk.astype(jnp.float32), precision=lax.Precision.HIGHEST)
        output_full = row_accum / row_total[:, None]
        deltas = lax.optimization_barrier(jnp.sum(grad_rows.astype(jnp.float32) * output_full, axis=1))
        probs = weights / row_total[:, None]
        probs_low = probs.astype(jnp.bfloat16)
        value_grad = jnp.dot(probs_low.T, grad_rows, preferred_element_type=jnp.float32)
        prob_grad = jnp.dot(grad_rows, value_blk.T, preferred_element_type=jnp.float32)
        score_grad = (probs * (prob_grad - deltas[:, None]) * score_scale).astype(jnp.bfloat16)
        query_grad = jnp.dot(score_grad, key_blk, preferred_element_type=jnp.float32)
        key_grad = jnp.dot(score_grad.T, query_rows, preferred_element_type=jnp.float32)
        term = jnp.concatenate([key_grad, value_grad], axis=1)
        old = lax.dynamic_slice_in_dim(grad_all, start, WINDOW)
        grad_all = lax.dynamic_update_slice_in_dim(grad_all, old + term, start, 0)
        out_rows = output_full.reshape(TOK_DEV, HQ * HD).astype(jnp.bfloat16)
        qgrad_rows = query_grad.reshape(TOK_DEV, HQ * HD).astype(jnp.bfloat16)
        return (grad_all, (out_rows, qgrad_rows))
    start_all = jnp.zeros((SEQ + lead, 2 * HD), jnp.float32)
    grad_all, (out_blocks, qgrad_blocks) = lax.scan(one_block, start_all, (block_ids, query_blocks, grad_blocks))
    attended = out_blocks.reshape(SEQ, HQ * HD)
    grad_queries = qgrad_blocks.reshape(SEQ, HQ * HD)
    owned = grad_all[lead:]
    grad_keys = owned[:, :HD].astype(jnp.bfloat16)
    grad_values = owned[:, HD:].astype(jnp.bfloat16)
    return (attended, grad_queries, grad_keys, grad_values)
```

```python
import math

import jax
import jax.numpy as jnp
from jax import lax
from jax.experimental import pallas as pl
from jax.experimental.pallas import tpu as pltpu
from jax.sharding import PartitionSpec as P

REACH = 8
HEADS = 8
MASKED = -1e30


def contract_last(left_op, right_op):
    return lax.dot_general(
        left_op, right_op, (((1,), (1,)), ((), ())), preferred_element_type=jnp.float32
    )


def contract_first(left_op, right_op):
    return lax.dot_general(
        left_op, right_op, (((0,), (0,)), ((), ())), preferred_element_type=jnp.float32
    )


def attention_kernel(me_ref, kv_ref, q_ref, g_ref, doc_ref, out_ref, dq_ref, send_ref, bias_ref, dk_ref, dv_ref):
    tokens, width = kv_ref.shape[1], kv_ref.shape[2] // 2
    span = REACH * tokens
    scale = 1.0 / math.sqrt(width)
    me = me_ref[0]
    mine = lax.rem(me, REACH)
    row = me - mine

    query_doc = jnp.broadcast_to(doc_ref[pl.ds(me, 1), :], (tokens, tokens)).T
    lane = lax.broadcasted_iota(jnp.int32, (tokens, tokens), 1)
    line = lax.broadcasted_iota(jnp.int32, (tokens, tokens), 0)
    for j in range(REACH):
        block = jnp.where(j <= mine, row + j, row - REACH + j)
        key_doc = doc_ref[pl.ds(jnp.maximum(block, 0), 1), :]
        reach = jnp.where(block < 0, -1, jnp.where(j == mine, 0, tokens))
        visible = (key_doc == query_doc) & (lane <= line + reach) & (reach >= 0)
        bias_ref[:, j * tokens : (j + 1) * tokens] = jnp.where(visible, 0.0, MASKED)

    keys = kv_ref[:, :, :width].reshape(span, width)
    values = kv_ref[:, :, width:].reshape(span, width)
    values_one = jnp.concatenate([values, jnp.ones_like(values)], axis=1)

    for h in range(HEADS):
        cols = slice(h * width, (h + 1) * width)
        query = q_ref[:, cols]
        scores = contract_last(query, keys) * (scale * math.log2(math.e)) + bias_ref[...]
        top = jnp.max(scores, axis=1, keepdims=True)
        weights = jnp.exp2(scores - top).astype(jnp.bfloat16)
        sums = jnp.dot(weights, values_one, preferred_element_type=jnp.float32)
        inverse = 1.0 / sums[:, width:]
        output = sums[:, :width] * inverse
        out_ref[:, cols] = output.astype(jnp.bfloat16)
        grad = (g_ref[:, cols].astype(jnp.float32) * (inverse * scale)).astype(jnp.bfloat16)
        delta = jnp.sum(grad.astype(jnp.float32) * output, axis=1, keepdims=True)
        slope = contract_last(grad, values) - delta
        score_grad = (weights.astype(jnp.float32) * slope).astype(jnp.bfloat16)
        dq_ref[:, cols] = jnp.dot(score_grad, keys, preferred_element_type=jnp.float32).astype(jnp.bfloat16)
        dk = contract_first(query, score_grad)
        dv = contract_first(grad, weights)
        if h == 0:
            dk_ref[...] = dk
            dv_ref[...] = dv
        else:
            dk_ref[...] += dk
            dv_ref[...] += dv

    for j in range(REACH):
        at = slice(j * tokens, (j + 1) * tokens)
        send_ref[j, :, :width] = dk_ref[:, at].T.astype(jnp.bfloat16)
        send_ref[j, :, width:] = (dv_ref[:, at].T * (1.0 / scale)).astype(jnp.bfloat16)


def attention(me, window, queries, d_out, docs):
    tokens, wide = queries.shape
    span = window.shape[0] * tokens
    width = window.shape[2] // 2
    vmem = pl.BlockSpec(memory_space=pltpu.VMEM)
    return pl.pallas_call(
        attention_kernel,
        out_shape=(
            jax.ShapeDtypeStruct((tokens, wide), jnp.bfloat16),
            jax.ShapeDtypeStruct((tokens, wide), jnp.bfloat16),
            jax.ShapeDtypeStruct(window.shape, jnp.bfloat16),
        ),
        in_specs=[pl.BlockSpec(memory_space=pltpu.SMEM), vmem, vmem, vmem, vmem],
        out_specs=(vmem, vmem, vmem),
        scratch_shapes=[
            pltpu.VMEM((tokens, span), jnp.float32),
            pltpu.VMEM((width, span), jnp.float32),
            pltpu.VMEM((width, span), jnp.float32),
        ],
        compiler_params=pltpu.CompilerParams(vmem_limit_bytes=40 * 1024 * 1024),
        cost_estimate=pl.CostEstimate(
            flops=12 * HEADS * tokens * span * width, bytes_accessed=3 * 1024 * 1024, transcendentals=HEADS * tokens * span
        ),
    )(me, window, queries, d_out, docs)


def body(queries, keys, values, d_out, doc_ids):
    axes = ("outer", "inner")
    n_inner = lax.axis_size("inner")
    total = lax.axis_size("outer") * n_inner
    me = lax.axis_index("outer") * n_inner + lax.axis_index("inner")
    mine = lax.rem(me, REACH)
    tokens, width = keys.shape
    lines = [[start + k for k in range(REACH)] for start in range(0, n_inner, REACH)]
    slot = jnp.arange(REACH, dtype=jnp.int32)[:, None, None]

    def exchange(parts):
        return lax.all_to_all(parts, "inner", 0, 0, axis_index_groups=lines)

    packed = jnp.concatenate([keys, values], axis=1)
    behind = lax.ppermute(packed, axes, [(i, i + REACH) for i in range(total - REACH)])
    window = exchange(jnp.where(slot >= mine, packed[None], behind[None]))
    attended, grad_queries, parts = attention(
        me.reshape(1), window, queries, d_out, doc_ids.reshape(-1, tokens)
    )
    terms = exchange(parts).astype(jnp.float32)
    passed = jnp.sum(jnp.where(slot < mine, terms, 0.0), axis=0).astype(jnp.bfloat16)
    passed = lax.ppermute(passed, axes, [(i, i - REACH) for i in range(REACH, total)])
    owned = jnp.sum(jnp.where(slot >= mine, terms, 0.0), axis=0) + passed.astype(jnp.float32)
    grad_keys = owned[:, :width].astype(jnp.bfloat16)
    grad_values = owned[:, width:].astype(jnp.bfloat16)
    return (attended, grad_queries, grad_keys, grad_values)


def solution(mesh):
    split = P(("outer", "inner"), None)
    return jax.shard_map(
        body,
        mesh=mesh,
        in_specs=(split, split, split, split, P()),
        out_specs=(split, split, split, split),
        check_vma=False,
    )
```

```python
import math

import jax
import jax.numpy as jnp
from jax import lax
from jax.experimental import pallas as pl
from jax.experimental.pallas import tpu as pltpu
from jax.sharding import PartitionSpec as P

REACH = 8
HEADS = 8
MASKED = -1e30
GATHER_ORDER = (5, 6, 7, 0, 1, 2, 3, 4)
RETURN_ORDER = (5, 6, 7, 0, 1, 2, 3, 4)


def contract_last(left_op, right_op):
    return lax.dot_general(
        left_op, right_op, (((1,), (1,)), ((), ())), preferred_element_type=jnp.float32
    )


def contract_first(left_op, right_op):
    return lax.dot_general(
        left_op, right_op, (((0,), (0,)), ((), ())), preferred_element_type=jnp.float32
    )


def pack_kernel(key_ref, value_ref, out_ref):
    width = key_ref.shape[1]
    out_ref[:, :width] = key_ref[...]
    out_ref[:, width:] = value_ref[...]


def attention_kernel(
    me_ref, kv_ref, q_ref, g_ref, doc_ref, out_ref, dq_ref, send_ref,
    bias_ref, w_ref, ds_ref, rows_ref, grads_ref,
):
    tokens, width = kv_ref.shape[1], kv_ref.shape[2] // 2
    span = REACH * tokens
    scale = 1.0 / math.sqrt(width)
    me = me_ref[0]
    mine = lax.rem(me, REACH)
    row = me - mine

    query_doc = jnp.broadcast_to(doc_ref[pl.ds(me, 1), :], (tokens, tokens)).T
    lane = lax.broadcasted_iota(jnp.int32, (tokens, tokens), 1)
    line = lax.broadcasted_iota(jnp.int32, (tokens, tokens), 0)
    for k, j in enumerate(GATHER_ORDER):
        block = jnp.where(j <= mine, row + j, row - REACH + j)
        key_doc = doc_ref[pl.ds(jnp.maximum(block, 0), 1), :]
        reach = jnp.where(block < 0, -tokens, jnp.where(j == mine, 0, tokens))
        visible = (key_doc == query_doc) & (lane <= line + reach)
        bias_ref[:, k * tokens : (k + 1) * tokens] = jnp.where(visible, 0.0, MASKED)

    keys = kv_ref[:, :, :width].reshape(span, width)
    values = kv_ref[:, :, width:].reshape(span, width)
    values_one = jnp.concatenate([values, jnp.ones_like(values)], axis=1)

    heads = [
        (slice(h * width, (h + 1) * width), slice(h * tokens, (h + 1) * tokens)) for h in range(HEADS)
    ]
    for cols, rows in heads:
        query = q_ref[:, cols]
        rows_ref[rows, :] = query
        scores = contract_last(query, keys) * (scale * math.log2(math.e)) + bias_ref[...]
        top = jnp.max(scores, axis=1, keepdims=True)
        w_ref[rows, :] = jnp.exp2(scores - top).astype(jnp.bfloat16)
    sums_all = jnp.dot(w_ref[...], values_one, preferred_element_type=jnp.float32)
    deltas = []
    for cols, rows in heads:
        inverse = 1.0 / sums_all[rows, width:]
        output = sums_all[rows, :width] * inverse
        out_ref[:, cols] = output.astype(jnp.bfloat16)
        grad = (g_ref[:, cols].astype(jnp.float32) * (inverse * scale)).astype(jnp.bfloat16)
        grads_ref[rows, :] = grad
        deltas.append(jnp.sum(grad.astype(jnp.float32) * output, axis=1, keepdims=True))
    for (cols, rows), delta in zip(heads, deltas):
        slope = contract_last(grads_ref[rows, :], values) - delta
        ds_ref[rows, :] = (w_ref[rows, :].astype(jnp.float32) * slope).astype(jnp.bfloat16)
    dq = jnp.dot(ds_ref[...], keys, preferred_element_type=jnp.float32).astype(jnp.bfloat16)
    for cols, rows in heads:
        dq_ref[:, cols] = dq[rows, :]
    dk = contract_first(rows_ref[...], ds_ref[...])
    dv = contract_first(grads_ref[...], w_ref[...])
    for k, j in enumerate(GATHER_ORDER):
        at = slice(k * tokens, (k + 1) * tokens)
        send_ref[RETURN_ORDER.index(j), :, :width] = dk[:, at].T.astype(jnp.bfloat16)
        send_ref[RETURN_ORDER.index(j), :, width:] = (dv[:, at].T * (1.0 / scale)).astype(jnp.bfloat16)


def attention(me, window, queries, d_out, docs):
    tokens, wide = queries.shape
    span = window.shape[0] * tokens
    width = window.shape[2] // 2
    vmem = pl.BlockSpec(memory_space=pltpu.VMEM)
    return pl.pallas_call(
        attention_kernel,
        out_shape=(
            jax.ShapeDtypeStruct((tokens, wide), jnp.bfloat16),
            jax.ShapeDtypeStruct((tokens, wide), jnp.bfloat16),
            jax.ShapeDtypeStruct(window.shape, jnp.bfloat16),
        ),
        in_specs=[pl.BlockSpec(memory_space=pltpu.SMEM), vmem, vmem, vmem, vmem],
        out_specs=(vmem, vmem, vmem),
        scratch_shapes=[
            pltpu.VMEM((tokens, span), jnp.float32),
            pltpu.VMEM((HEADS * tokens, span), jnp.bfloat16),
            pltpu.VMEM((HEADS * tokens, span), jnp.bfloat16),
            pltpu.VMEM((HEADS * tokens, width), jnp.bfloat16),
            pltpu.VMEM((HEADS * tokens, width), jnp.bfloat16),
        ],
        compiler_params=pltpu.CompilerParams(vmem_limit_bytes=40 * 1024 * 1024),
        cost_estimate=pl.CostEstimate(
            flops=12 * HEADS * tokens * span * width,
            bytes_accessed=3 * 1024 * 1024,
            transcendentals=HEADS * tokens * span,
        ),
    )(me, window, queries, d_out, docs)


def body(queries, keys, values, d_out, doc_ids):
    axes = ("outer", "inner")
    n_inner = lax.axis_size("inner")
    total = lax.axis_size("outer") * n_inner
    me = lax.axis_index("outer") * n_inner + lax.axis_index("inner")
    mine = lax.rem(me, REACH)
    tokens, width = keys.shape

    def exchange(parts, order):
        lines = [[start + k for k in order] for start in range(0, n_inner, REACH)]
        return lax.all_to_all(parts, "inner", 0, 0, axis_index_groups=lines)

    def partner(order):
        return jnp.array(order, dtype=jnp.int32)[:, None, None]

    packed = jnp.concatenate([keys, values], axis=1)
    behind = lax.ppermute(packed, axes, [(i, i + REACH) for i in range(total - REACH)])
    outgoing = jnp.where(partner(GATHER_ORDER) >= mine, packed[None], behind[None])
    window = exchange(outgoing, GATHER_ORDER)
    attended, grad_queries, parts = attention(
        me.reshape(1), window, queries, d_out, doc_ids.reshape(-1, tokens)
    )
    terms = exchange(parts, RETURN_ORDER).astype(jnp.float32)
    ahead = partner(RETURN_ORDER) < mine
    passed = jnp.sum(jnp.where(ahead, terms, 0.0), axis=0).astype(jnp.bfloat16)
    passed = lax.ppermute(passed, axes, [(i, i - REACH) for i in range(REACH, total)])
    owned = jnp.sum(jnp.where(ahead, 0.0, terms), axis=0) + passed.astype(jnp.float32)
    grad_keys = owned[:, :width].astype(jnp.bfloat16)
    grad_values = owned[:, width:].astype(jnp.bfloat16)
    return (attended, grad_queries, grad_keys, grad_values)


def solution(mesh):
    split = P(("outer", "inner"), None)
    return jax.shard_map(
        body,
        mesh=mesh,
        in_specs=(split, split, split, split, P()),
        out_specs=(split, split, split, split),
        check_vma=False,
    )
```

```python
import math

import jax
import jax.numpy as jnp
from jax import lax
from jax.experimental import pallas as pl
from jax.experimental.pallas import tpu as pltpu
from jax.sharding import PartitionSpec as P

REACH = 8
HEADS = 8
MASKED = -1e30
FIRST = 5
ORDER = tuple((FIRST + k) % REACH for k in range(REACH))
AXES = ("outer", "inner")
MIB = 1024 * 1024
VMEM = pl.BlockSpec(memory_space=pltpu.VMEM)
HBM = pl.BlockSpec(memory_space=pltpu.HBM)


def contract_last(left_op, right_op):
    return lax.dot_general(
        left_op, right_op, (((1,), (1,)), ((), ())), preferred_element_type=jnp.float32
    )


def contract_first(left_op, right_op):
    return lax.dot_general(
        left_op, right_op, (((0,), (0,)), ((), ())), preferred_element_type=jnp.float32
    )


def position():
    me = lax.axis_index("outer") * lax.axis_size("inner") + lax.axis_index("inner")
    return me, lax.rem(me, REACH)


def prepare_kernel(
    k_ref, v_ref, q_ref, g_ref, doc_ref, pack_ref, bias_ref, queries_ref, grads_ref, docs_ref, sems
):
    tokens, width = k_ref.shape
    me, mine = position()
    row = me - mine
    first = pl.multiple_of(jnp.maximum(row - REACH, 0), REACH)
    copies = [
        pltpu.make_async_copy(doc_ref.at[pl.ds(first, 2 * REACH), :], docs_ref, sems.at[0]),
        pltpu.make_async_copy(k_ref, pack_ref.at[:, :width], sems.at[1]),
        pltpu.make_async_copy(v_ref, pack_ref.at[:, width:], sems.at[2]),
        pltpu.make_async_copy(q_ref, queries_ref, sems.at[3]),
        pltpu.make_async_copy(g_ref, grads_ref, sems.at[4]),
    ]
    for copy in copies:
        copy.start()
    lane = lax.broadcasted_iota(jnp.int32, (tokens, tokens), 1)
    line = lax.broadcasted_iota(jnp.int32, (tokens, tokens), 0)
    copies[0].wait()
    query_doc = jnp.broadcast_to(docs_ref[pl.ds(me - first, 1), :], (tokens, tokens)).T
    for k, j in enumerate(ORDER):
        block = jnp.where(j <= mine, row + j, row - REACH + j)
        key_doc = docs_ref[pl.ds(jnp.maximum(block, 0) - first, 1), :]
        reach = jnp.where(block < 0, -tokens, jnp.where(j == mine, 0, tokens))
        visible = (key_doc == query_doc) & (lane <= line + reach)
        bias_ref[:, k * tokens : (k + 1) * tokens] = jnp.where(visible, 0.0, MASKED)
    for copy in copies[1:]:
        copy.wait()


def prepare(keys, values, queries, d_out, docs):
    tokens, width = keys.shape
    return pl.pallas_call(
        prepare_kernel,
        out_shape=(
            pltpu.VMEM((tokens, 2 * width), jnp.bfloat16),
            pltpu.VMEM((tokens, REACH * tokens), jnp.float32),
            pltpu.VMEM(queries.shape, jnp.bfloat16),
            pltpu.VMEM(d_out.shape, jnp.bfloat16),
        ),
        in_specs=[HBM] * 5,
        out_specs=(VMEM,) * 4,
        scratch_shapes=[
            pltpu.VMEM((2 * REACH, tokens), jnp.int32),
            pltpu.SemaphoreType.DMA((5,)),
        ],
        compiler_params=pltpu.CompilerParams(vmem_limit_bytes=16 * MIB),
    )(*[pltpu.with_memory_space_constraint(a, pltpu.HBM) for a in (keys, values, queries, d_out, docs)])


def route_kernel(own_ref, behind_ref, out_ref):
    _, mine = position()
    for k, j in enumerate(ORDER):

        @pl.when(j >= mine)
        def _():
            out_ref[k] = own_ref[...]

        @pl.when(j < mine)
        def _():
            out_ref[k] = behind_ref[...]


def route(own, behind):
    return pl.pallas_call(
        route_kernel,
        out_shape=pltpu.VMEM((REACH, *own.shape), own.dtype),
        in_specs=[VMEM, VMEM],
        out_specs=VMEM,
        compiler_params=pltpu.CompilerParams(vmem_limit_bytes=16 * MIB),
    )(own, behind)


def attention_kernel(
    kv_ref, q_ref, g_ref, bias_ref, out_ref, ds_ref, send_ref, w_ref, rows_ref, grads_ref
):
    tokens, width = kv_ref.shape[1], kv_ref.shape[2] // 2
    span = REACH * tokens
    scale = 1.0 / math.sqrt(width)

    keys = kv_ref[:, :, :width].reshape(span, width)
    values = kv_ref[:, :, width:].reshape(span, width)
    values_one = jnp.concatenate([values, jnp.ones_like(values)], axis=1)

    heads = [
        (slice(h * width, (h + 1) * width), slice(h * tokens, (h + 1) * tokens)) for h in range(HEADS)
    ]
    for cols, rows in heads:
        query = q_ref[:, cols]
        rows_ref[rows, :] = query
        scores = contract_last(query, keys) * (scale * math.log2(math.e)) + bias_ref[...]
        top = jnp.max(scores, axis=1, keepdims=True)
        w_ref[rows, :] = jnp.exp2(scores - top).astype(jnp.bfloat16)
    sums_all = jnp.dot(w_ref[...], values_one, preferred_element_type=jnp.float32)
    deltas = []
    for cols, rows in heads:
        inverse = 1.0 / sums_all[rows, width:]
        output = sums_all[rows, :width] * inverse
        out_ref[:, cols] = output.astype(jnp.bfloat16)
        grad = (g_ref[:, cols].astype(jnp.float32) * (inverse * scale)).astype(jnp.bfloat16)
        grads_ref[rows, :] = grad
        deltas.append(jnp.sum(grad.astype(jnp.float32) * output, axis=1, keepdims=True))
    for (cols, rows), delta in zip(heads, deltas):
        slope = contract_last(grads_ref[rows, :], values) - delta
        ds_ref[rows, :] = (w_ref[rows, :].astype(jnp.float32) * slope).astype(jnp.bfloat16)
    dk = contract_first(rows_ref[...], ds_ref[...])
    dv = contract_first(grads_ref[...], w_ref[...])
    for k in range(REACH):
        at = slice(k * tokens, (k + 1) * tokens)
        send_ref[k, :, :width] = dk[:, at].T.astype(jnp.bfloat16)
        send_ref[k, :, width:] = (dv[:, at].T * (1.0 / scale)).astype(jnp.bfloat16)


def attention(window, queries, d_out, bias):
    tokens, wide = queries.shape
    span = window.shape[0] * tokens
    width = window.shape[2] // 2
    return pl.pallas_call(
        attention_kernel,
        out_shape=(
            jax.ShapeDtypeStruct((tokens, wide), jnp.bfloat16),
            pltpu.VMEM((HEADS * tokens, span), jnp.bfloat16),
            jax.ShapeDtypeStruct(window.shape, jnp.bfloat16),
        ),
        in_specs=[VMEM] * 4,
        out_specs=(VMEM,) * 3,
        scratch_shapes=[
            pltpu.VMEM((HEADS * tokens, span), jnp.bfloat16),
            pltpu.VMEM((HEADS * tokens, width), jnp.bfloat16),
            pltpu.VMEM((HEADS * tokens, width), jnp.bfloat16),
        ],
        compiler_params=pltpu.CompilerParams(vmem_limit_bytes=40 * MIB),
        cost_estimate=pl.CostEstimate(
            flops=10 * HEADS * tokens * span * width,
            bytes_accessed=3 * MIB,
            transcendentals=HEADS * tokens * span,
        ),
    )(window, queries, d_out, bias)


def query_kernel(ds_ref, kv_ref, dq_ref):
    tokens, width = kv_ref.shape[1], kv_ref.shape[2] // 2
    keys = kv_ref[:, :, :width].reshape(REACH * tokens, width)
    dq = jnp.dot(ds_ref[...], keys, preferred_element_type=jnp.float32).astype(jnp.bfloat16)
    for h in range(HEADS):
        dq_ref[:, h * width : (h + 1) * width] = dq[h * tokens : (h + 1) * tokens, :]


def query_grad(score_grad, window):
    tokens, width = window.shape[1], window.shape[2] // 2
    return pl.pallas_call(
        query_kernel,
        out_shape=jax.ShapeDtypeStruct((tokens, HEADS * width), jnp.bfloat16),
        in_specs=[VMEM, VMEM],
        out_specs=VMEM,
        compiler_params=pltpu.CompilerParams(vmem_limit_bytes=16 * MIB),
        cost_estimate=pl.CostEstimate(
            flops=2 * HEADS * tokens * REACH * tokens * width, bytes_accessed=3 * MIB, transcendentals=0
        ),
    )(score_grad, window)


def gather_kernel(terms_ref, passed_ref, owned_ref):
    _, mine = position()
    passed = jnp.zeros(passed_ref.shape, jnp.float32)
    owned = jnp.zeros(owned_ref.shape, jnp.float32)
    for k, j in enumerate(ORDER):
        term = terms_ref[k].astype(jnp.float32)
        passed = passed + jnp.where(j < mine, term, 0.0)
        owned = owned + jnp.where(j < mine, 0.0, term)
    passed_ref[...] = passed.astype(jnp.bfloat16)
    owned_ref[...] = owned


def gather(terms):
    return pl.pallas_call(
        gather_kernel,
        out_shape=(pltpu.VMEM(terms.shape[1:], jnp.bfloat16), pltpu.VMEM(terms.shape[1:], jnp.float32)),
        in_specs=[VMEM],
        out_specs=(VMEM, VMEM),
        compiler_params=pltpu.CompilerParams(vmem_limit_bytes=16 * MIB),
    )(terms)


def body(queries, keys, values, d_out, doc_ids):
    n_inner = lax.axis_size("inner")
    total = lax.axis_size("outer") * n_inner
    tokens, width = keys.shape
    lines = [[start + j for j in ORDER] for start in range(0, n_inner, REACH)]

    def exchange(parts):
        return lax.all_to_all(parts, "inner", 0, 0, axis_index_groups=lines)

    packed, bias, queries, d_out = prepare(keys, values, queries, d_out, doc_ids.reshape(-1, tokens))
    behind = lax.ppermute(packed, AXES, [(i, i + REACH) for i in range(total - REACH)])
    window = exchange(route(packed, behind))
    attended, score_grad, parts = attention(window, queries, d_out, bias)
    passed, owned = gather(exchange(parts))
    passed = lax.ppermute(passed, AXES, [(i, i - REACH) for i in range(REACH, total)])
    grad_queries = query_grad(score_grad, window)
    owned = (owned + passed.astype(jnp.float32)).astype(jnp.bfloat16)
    return (attended, grad_queries, owned[:, :width], owned[:, width:])


def solution(mesh):
    split = P(("outer", "inner"), None)
    return jax.shard_map(
        body,
        mesh=mesh,
        in_specs=(split, split, split, split, P()),
        out_specs=(split, split, split, split),
        check_vma=False,
    )
```

```python
import math

import jax
import jax.numpy as jnp
from jax import lax
from jax.experimental import pallas as pl
from jax.experimental.pallas import tpu as pltpu
from jax.sharding import PartitionSpec as P

REACH = 8
HEADS = 8
MASKED = -1e30
FIRST = 5
ORDER = tuple((FIRST + k) % REACH for k in range(REACH))
AXES = ("outer", "inner")
MIB = 1024 * 1024
VMEM = pl.BlockSpec(memory_space=pltpu.VMEM)
HBM = pl.BlockSpec(memory_space=pltpu.HBM)


def contract_last(left_op, right_op):
    return lax.dot_general(
        left_op, right_op, (((1,), (1,)), ((), ())), preferred_element_type=jnp.float32
    )


def contract_first(left_op, right_op):
    return lax.dot_general(
        left_op, right_op, (((0,), (0,)), ((), ())), preferred_element_type=jnp.float32
    )


def position():
    me = lax.axis_index("outer") * lax.axis_size("inner") + lax.axis_index("inner")
    return me, lax.rem(me, REACH)


def on_first_core():
    return lax.rem(lax.axis_index("outer"), 2) == 0


def pack_kernel(k_ref, v_ref, pack_ref, sems):
    width = k_ref.shape[1]
    copies = [
        pltpu.make_async_copy(k_ref, pack_ref.at[:, :width], sems.at[0]),
        pltpu.make_async_copy(v_ref, pack_ref.at[:, width:], sems.at[1]),
    ]
    for copy in copies:
        copy.start()
    for copy in copies:
        copy.wait()


def pack(keys, values):
    tokens, width = keys.shape
    return pl.pallas_call(
        pack_kernel,
        out_shape=pltpu.VMEM((tokens, 2 * width), jnp.bfloat16),
        in_specs=[HBM] * 2,
        out_specs=VMEM,
        scratch_shapes=[pltpu.SemaphoreType.DMA((2,))],
        compiler_params=pltpu.CompilerParams(vmem_limit_bytes=16 * MIB),
    )(*[pltpu.with_memory_space_constraint(a, pltpu.HBM) for a in (keys, values)])


def stage(q_ref, g_ref, doc_ref, bias_ref, queries_ref, grads_ref, turned_ref, docs_ref, sems):
    tokens = bias_ref.shape[0]
    me, mine = position()
    row = me - mine
    first = pl.multiple_of(jnp.maximum(row - REACH, 0), REACH)
    copies = [
        pltpu.make_async_copy(doc_ref.at[pl.ds(first, 2 * REACH), :], docs_ref, sems.at[0]),
        pltpu.make_async_copy(q_ref, queries_ref, sems.at[1]),
        pltpu.make_async_copy(g_ref, grads_ref, sems.at[2]),
    ]
    for copy in copies:
        copy.start()
    lane = lax.broadcasted_iota(jnp.int32, (tokens, tokens), 1)
    line = lax.broadcasted_iota(jnp.int32, (tokens, tokens), 0)
    copies[0].wait()
    query_doc = jnp.broadcast_to(docs_ref[pl.ds(me - first, 1), :], (tokens, tokens)).T
    for k, j in enumerate(ORDER):
        block = jnp.where(j <= mine, row + j, row - REACH + j)
        key_doc = docs_ref[pl.ds(jnp.maximum(block, 0) - first, 1), :]
        reach = jnp.where(block < 0, -tokens, jnp.where(j == mine, 0, tokens))
        visible = (key_doc == query_doc) & (lane <= line + reach)
        bias_ref[:, k * tokens : (k + 1) * tokens] = jnp.where(visible, 0.0, MASKED)
    for copy in copies[1:]:
        copy.wait()
    width = turned_ref.shape[0]
    for h in range(HEADS):
        turned_ref[:, h * tokens : (h + 1) * tokens] = queries_ref[:, h * width : (h + 1) * width].T


def prepare_kernel(*refs):
    @pl.when(jnp.logical_not(on_first_core()))
    def _():
        stage(*refs)


def prepare(queries, d_out, docs):
    tokens = queries.shape[0]
    return pl.pallas_call(
        prepare_kernel,
        out_shape=(
            pltpu.VMEM((tokens, REACH * tokens), jnp.float32),
            pltpu.VMEM(queries.shape, jnp.bfloat16),
            pltpu.VMEM(d_out.shape, jnp.bfloat16),
            pltpu.VMEM((queries.shape[1] // HEADS, HEADS * tokens), jnp.bfloat16),
        ),
        in_specs=[HBM] * 3,
        out_specs=(VMEM,) * 4,
        scratch_shapes=[
            pltpu.VMEM((2 * REACH, tokens), jnp.int32),
            pltpu.SemaphoreType.DMA((3,)),
        ],
        compiler_params=pltpu.CompilerParams(vmem_limit_bytes=16 * MIB),
    )(*[pltpu.with_memory_space_constraint(a, pltpu.HBM) for a in (queries, d_out, docs)])


def route_kernel(own_ref, behind_ref, q_ref, g_ref, doc_ref, b_in, q_in, g_in, t_in, out_ref, *refs):
    _, mine = position()
    for k, j in enumerate(ORDER):

        @pl.when(j >= mine)
        def _():
            out_ref[k] = own_ref[...]

        @pl.when(j < mine)
        def _():
            out_ref[k] = behind_ref[...]

    @pl.when(on_first_core())
    def _():
        stage(q_ref, g_ref, doc_ref, *refs)


def route(own, behind, queries, d_out, docs, staged):
    tokens = own.shape[0]
    return pl.pallas_call(
        route_kernel,
        out_shape=(
            pltpu.VMEM((REACH, *own.shape), own.dtype),
            *[pltpu.VMEM(a.shape, a.dtype) for a in staged],
        ),
        in_specs=[VMEM] * 2 + [HBM] * 3 + [VMEM] * 4,
        out_specs=(VMEM,) * 5,
        input_output_aliases={5: 1, 6: 2, 7: 3, 8: 4},
        scratch_shapes=[
            pltpu.VMEM((2 * REACH, tokens), jnp.int32),
            pltpu.SemaphoreType.DMA((3,)),
        ],
        compiler_params=pltpu.CompilerParams(vmem_limit_bytes=16 * MIB),
    )(own, behind, *[pltpu.with_memory_space_constraint(a, pltpu.HBM) for a in (queries, d_out, docs)], *staged)


def attention_kernel(
    kv_ref, q_ref, g_ref, bias_ref, turned_ref, out_ref, ds_ref, send_ref, w_ref, grads_ref
):
    tokens, width = kv_ref.shape[1], kv_ref.shape[2] // 2
    span = REACH * tokens
    scale = 1.0 / math.sqrt(width)

    keys = kv_ref[:, :, :width].reshape(span, width)
    values = kv_ref[:, :, width:].reshape(span, width)
    values_one = jnp.concatenate([values, jnp.ones_like(values)], axis=1)

    heads = [
        (slice(h * width, (h + 1) * width), slice(h * tokens, (h + 1) * tokens)) for h in range(HEADS)
    ]
    for cols, rows in heads:
        query = q_ref[:, cols]
        scores = contract_last(query, keys) * (scale * math.log2(math.e)) + bias_ref[...]
        top = jnp.max(scores, axis=1, keepdims=True)
        w_ref[rows, :] = jnp.exp2(scores - top).astype(jnp.bfloat16)
    sums_all = jnp.dot(w_ref[...], values_one, preferred_element_type=jnp.float32)
    deltas = []
    for cols, rows in heads:
        inverse = 1.0 / sums_all[rows, width:]
        output = sums_all[rows, :width] * inverse
        out_ref[:, cols] = output.astype(jnp.bfloat16)
        grad = (g_ref[:, cols].astype(jnp.float32) * (inverse * scale)).astype(jnp.bfloat16)
        grads_ref[rows, :] = grad
        deltas.append(jnp.sum(grad.astype(jnp.float32) * output, axis=1, keepdims=True))
    for (cols, rows), delta in zip(heads, deltas):
        slope = contract_last(grads_ref[rows, :], values) - delta
        ds_ref[rows, :] = (w_ref[rows, :].astype(jnp.float32) * slope).astype(jnp.bfloat16)
    dk = jnp.dot(turned_ref[...], ds_ref[...], preferred_element_type=jnp.float32)
    dv = contract_first(grads_ref[...], w_ref[...])
    for k in range(REACH):
        at = slice(k * tokens, (k + 1) * tokens)
        send_ref[k, :, :width] = dk[:, at].T.astype(jnp.bfloat16)
        send_ref[k, :, width:] = (dv[:, at].T * (1.0 / scale)).astype(jnp.bfloat16)


def attention(window, queries, d_out, bias, turned):
    tokens, wide = queries.shape
    span = window.shape[0] * tokens
    width = window.shape[2] // 2
    return pl.pallas_call(
        attention_kernel,
        out_shape=(
            jax.ShapeDtypeStruct((tokens, wide), jnp.bfloat16),
            pltpu.VMEM((HEADS * tokens, span), jnp.bfloat16),
            jax.ShapeDtypeStruct(window.shape, jnp.bfloat16),
        ),
        in_specs=[VMEM] * 5,
        out_specs=(VMEM,) * 3,
        scratch_shapes=[
            pltpu.VMEM((HEADS * tokens, span), jnp.bfloat16),
            pltpu.VMEM((HEADS * tokens, width), jnp.bfloat16),
        ],
        compiler_params=pltpu.CompilerParams(vmem_limit_bytes=40 * MIB),
        cost_estimate=pl.CostEstimate(
            flops=10 * HEADS * tokens * span * width,
            bytes_accessed=3 * MIB,
            transcendentals=HEADS * tokens * span,
        ),
    )(window, queries, d_out, bias, turned)


def query_kernel(ds_ref, kv_ref, dq_ref):
    tokens, width = kv_ref.shape[1], kv_ref.shape[2] // 2
    keys = kv_ref[:, :, :width].reshape(REACH * tokens, width)
    dq = jnp.dot(ds_ref[...], keys, preferred_element_type=jnp.float32).astype(jnp.bfloat16)
    for h in range(HEADS):
        dq_ref[:, h * width : (h + 1) * width] = dq[h * tokens : (h + 1) * tokens, :]


def query_grad(score_grad, window):
    tokens, width = window.shape[1], window.shape[2] // 2
    return pl.pallas_call(
        query_kernel,
        out_shape=jax.ShapeDtypeStruct((tokens, HEADS * width), jnp.bfloat16),
        in_specs=[VMEM] * 2,
        out_specs=VMEM,
        compiler_params=pltpu.CompilerParams(vmem_limit_bytes=16 * MIB),
        cost_estimate=pl.CostEstimate(
            flops=2 * HEADS * tokens * REACH * tokens * width, bytes_accessed=3 * MIB, transcendentals=0
        ),
    )(score_grad, window)


def gather_kernel(terms_ref, passed_ref, owned_ref):
    _, mine = position()
    passed = jnp.zeros(passed_ref.shape, jnp.float32)
    owned = jnp.zeros(owned_ref.shape, jnp.float32)
    for k, j in enumerate(ORDER):
        term = terms_ref[k].astype(jnp.float32)
        passed = passed + jnp.where(j < mine, term, 0.0)
        owned = owned + jnp.where(j < mine, 0.0, term)
    passed_ref[...] = passed.astype(jnp.bfloat16)
    owned_ref[...] = owned


def gather(terms):
    return pl.pallas_call(
        gather_kernel,
        out_shape=(pltpu.VMEM(terms.shape[1:], jnp.bfloat16), pltpu.VMEM(terms.shape[1:], jnp.float32)),
        in_specs=[VMEM],
        out_specs=(VMEM, VMEM),
        compiler_params=pltpu.CompilerParams(vmem_limit_bytes=16 * MIB),
    )(terms)


def body(queries, keys, values, d_out, doc_ids):
    n_inner = lax.axis_size("inner")
    total = lax.axis_size("outer") * n_inner
    tokens, width = keys.shape
    lines = [[start + j for j in ORDER] for start in range(0, n_inner, REACH)]

    def exchange(parts):
        return lax.all_to_all(parts, "inner", 0, 0, axis_index_groups=lines)

    packed = pack(keys, values)
    behind = lax.ppermute(packed, AXES, [(i, i + REACH) for i in range(total - REACH)])
    docs = doc_ids.reshape(-1, tokens)
    staged = prepare(queries, d_out, docs)
    behind, *staged = lax.optimization_barrier((behind, *staged))
    outgoing, bias, rows, grads, turned = route(packed, behind, queries, d_out, docs, staged)
    window = exchange(outgoing)
    attended, score_grad, parts = attention(window, rows, grads, bias, turned)
    passed, owned = gather(exchange(parts))
    passed = lax.ppermute(passed, AXES, [(i, i - REACH) for i in range(REACH, total)])
    grad_queries = query_grad(score_grad, window)
    owned = (owned + passed.astype(jnp.float32)).astype(jnp.bfloat16)
    return (attended, grad_queries, owned[:, :width], owned[:, width:])


def solution(mesh):
    split = P(("outer", "inner"), None)
    return jax.shard_map(
        body,
        mesh=mesh,
        in_specs=(split, split, split, split, P()),
        out_specs=(split, split, split, split),
        check_vma=False,
    )
```

```python
import math

import jax
import jax.numpy as jnp
from jax import lax
from jax.experimental import pallas as pl
from jax.experimental.pallas import tpu as pltpu
from jax.sharding import PartitionSpec as P

REACH = 8
HEADS = 8
MASKED = -1e30
FIRST = 5
ORDER = tuple((FIRST + k) % REACH for k in range(REACH))
AXES = ("outer", "inner")
MIB = 1024 * 1024
VMEM = pl.BlockSpec(memory_space=pltpu.VMEM)
HBM = pl.BlockSpec(memory_space=pltpu.HBM)


def contract_last(left_op, right_op):
    return lax.dot_general(
        left_op, right_op, (((1,), (1,)), ((), ())), preferred_element_type=jnp.float32
    )


def contract_first(left_op, right_op):
    return lax.dot_general(
        left_op, right_op, (((0,), (0,)), ((), ())), preferred_element_type=jnp.float32
    )


def position():
    me = lax.axis_index("outer") * lax.axis_size("inner") + lax.axis_index("inner")
    return me, lax.rem(me, REACH)


def on_first_core():
    return lax.rem(lax.axis_index("outer"), 2) == 0


def pack_kernel(k_ref, v_ref, pack_ref, sems):
    width = k_ref.shape[1]
    copies = [
        pltpu.make_async_copy(k_ref, pack_ref.at[:, :width], sems.at[0]),
        pltpu.make_async_copy(v_ref, pack_ref.at[:, width:], sems.at[1]),
    ]
    for copy in copies:
        copy.start()
    for copy in copies:
        copy.wait()


def pack(keys, values):
    tokens, width = keys.shape
    return pl.pallas_call(
        pack_kernel,
        out_shape=pltpu.VMEM((tokens, 2 * width), jnp.bfloat16),
        in_specs=[HBM] * 2,
        out_specs=VMEM,
        scratch_shapes=[pltpu.SemaphoreType.DMA((2,))],
        compiler_params=pltpu.CompilerParams(vmem_limit_bytes=16 * MIB),
    )(*[pltpu.with_memory_space_constraint(a, pltpu.HBM) for a in (keys, values)])


def stage(q_ref, g_ref, doc_ref, bias_ref, queries_ref, grads_ref, turned_ref, docs_ref, sems):
    tokens = bias_ref.shape[0]
    me, mine = position()
    row = me - mine
    first = pl.multiple_of(jnp.maximum(row - REACH, 0), REACH)
    copies = [
        pltpu.make_async_copy(doc_ref.at[pl.ds(first, 2 * REACH), :], docs_ref, sems.at[0]),
        pltpu.make_async_copy(q_ref, queries_ref, sems.at[1]),
        pltpu.make_async_copy(g_ref, grads_ref, sems.at[2]),
    ]
    for copy in copies:
        copy.start()
    lane = lax.broadcasted_iota(jnp.int32, (tokens, tokens), 1)
    line = lax.broadcasted_iota(jnp.int32, (tokens, tokens), 0)
    copies[0].wait()
    query_doc = jnp.broadcast_to(docs_ref[pl.ds(me - first, 1), :], (tokens, tokens)).T
    for k, j in enumerate(ORDER):
        block = jnp.where(j <= mine, row + j, row - REACH + j)
        key_doc = docs_ref[pl.ds(jnp.maximum(block, 0) - first, 1), :]
        reach = jnp.where(block < 0, -tokens, jnp.where(j == mine, 0, tokens))
        visible = (key_doc == query_doc) & (lane <= line + reach)
        bias_ref[:, k * tokens : (k + 1) * tokens] = jnp.where(visible, 0.0, MASKED)
    for copy in copies[1:]:
        copy.wait()
    width = turned_ref.shape[0]
    for h in range(HEADS):
        turned_ref[:, h * tokens : (h + 1) * tokens] = queries_ref[:, h * width : (h + 1) * width].T


def prepare_kernel(*refs):
    @pl.when(jnp.logical_not(on_first_core()))
    def _():
        stage(*refs)


def prepare(queries, d_out, docs):
    tokens = queries.shape[0]
    return pl.pallas_call(
        prepare_kernel,
        out_shape=(
            pltpu.VMEM((tokens, REACH * tokens), jnp.float32),
            pltpu.VMEM(queries.shape, jnp.bfloat16),
            pltpu.VMEM(d_out.shape, jnp.bfloat16),
            pltpu.VMEM((queries.shape[1] // HEADS, HEADS * tokens), jnp.bfloat16),
        ),
        in_specs=[HBM] * 3,
        out_specs=(VMEM,) * 4,
        scratch_shapes=[
            pltpu.VMEM((2 * REACH, tokens), jnp.int32),
            pltpu.SemaphoreType.DMA((3,)),
        ],
        compiler_params=pltpu.CompilerParams(vmem_limit_bytes=16 * MIB),
    )(*[pltpu.with_memory_space_constraint(a, pltpu.HBM) for a in (queries, d_out, docs)])


def route_kernel(own_ref, behind_ref, q_ref, g_ref, doc_ref, b_in, q_in, g_in, t_in, out_ref, *refs):
    _, mine = position()
    for k, j in enumerate(ORDER):

        @pl.when(j >= mine)
        def _():
            out_ref[k] = own_ref[...]

        @pl.when(j < mine)
        def _():
            out_ref[k] = behind_ref[...]

    @pl.when(on_first_core())
    def _():
        stage(q_ref, g_ref, doc_ref, *refs)


def route(own, behind, queries, d_out, docs, staged):
    tokens = own.shape[0]
    return pl.pallas_call(
        route_kernel,
        out_shape=(
            pltpu.VMEM((REACH, *own.shape), own.dtype),
            *[pltpu.VMEM(a.shape, a.dtype) for a in staged],
        ),
        in_specs=[VMEM] * 2 + [HBM] * 3 + [VMEM] * 4,
        out_specs=(VMEM,) * 5,
        input_output_aliases={5: 1, 6: 2, 7: 3, 8: 4},
        scratch_shapes=[
            pltpu.VMEM((2 * REACH, tokens), jnp.int32),
            pltpu.SemaphoreType.DMA((3,)),
        ],
        compiler_params=pltpu.CompilerParams(vmem_limit_bytes=16 * MIB),
    )(own, behind, *[pltpu.with_memory_space_constraint(a, pltpu.HBM) for a in (queries, d_out, docs)], *staged)


def attention_kernel(
    kv_ref, q_ref, g_ref, bias_ref, turned_ref, out_ref, ds_ref, send_ref, w_ref, grads_ref, flipped_ref
):
    tokens, width = kv_ref.shape[1], kv_ref.shape[2] // 2
    span = REACH * tokens
    scale = 1.0 / math.sqrt(width)

    keys = kv_ref[:, :, :width].reshape(span, width)
    values = kv_ref[:, :, width:].reshape(span, width)
    values_one = jnp.concatenate([values, jnp.ones_like(values)], axis=1)

    heads = [
        (slice(h * width, (h + 1) * width), slice(h * tokens, (h + 1) * tokens)) for h in range(HEADS)
    ]
    for cols, rows in heads:
        query = q_ref[:, cols]
        scores = contract_last(query, keys) * (scale * math.log2(math.e)) + bias_ref[...]
        top = jnp.max(scores, axis=1, keepdims=True)
        w_ref[rows, :] = jnp.exp2(scores - top).astype(jnp.bfloat16)
    sums_all = jnp.dot(w_ref[...], values_one, preferred_element_type=jnp.float32)
    deltas = []
    for cols, rows in heads:
        inverse = 1.0 / sums_all[rows, width:]
        output = sums_all[rows, :width] * inverse
        out_ref[:, cols] = output.astype(jnp.bfloat16)
        grad = (g_ref[:, cols].astype(jnp.float32) * (inverse * scale)).astype(jnp.bfloat16)
        grads_ref[rows, :] = grad
        flipped_ref[:, rows] = grad.T
        deltas.append(jnp.sum(grad.astype(jnp.float32) * output, axis=1, keepdims=True))
    for (cols, rows), delta in zip(heads, deltas):
        slope = contract_last(grads_ref[rows, :], values) - delta
        ds_ref[rows, :] = (w_ref[rows, :].astype(jnp.float32) * slope).astype(jnp.bfloat16)
    dk = jnp.dot(turned_ref[...], ds_ref[...], preferred_element_type=jnp.float32)
    dv = jnp.dot(flipped_ref[...], w_ref[...], preferred_element_type=jnp.float32)
    for k in range(REACH):
        at = slice(k * tokens, (k + 1) * tokens)
        send_ref[k, :, :width] = dk[:, at].T.astype(jnp.bfloat16)
        send_ref[k, :, width:] = (dv[:, at].T * (1.0 / scale)).astype(jnp.bfloat16)


def attention(window, queries, d_out, bias, turned):
    tokens, wide = queries.shape
    span = window.shape[0] * tokens
    width = window.shape[2] // 2
    return pl.pallas_call(
        attention_kernel,
        out_shape=(
            jax.ShapeDtypeStruct((tokens, wide), jnp.bfloat16),
            pltpu.VMEM((HEADS * tokens, span), jnp.bfloat16),
            jax.ShapeDtypeStruct(window.shape, jnp.bfloat16),
        ),
        in_specs=[VMEM] * 5,
        out_specs=(VMEM,) * 3,
        scratch_shapes=[
            pltpu.VMEM((HEADS * tokens, span), jnp.bfloat16),
            pltpu.VMEM((HEADS * tokens, width), jnp.bfloat16),
            pltpu.VMEM((width, HEADS * tokens), jnp.bfloat16),
        ],
        compiler_params=pltpu.CompilerParams(vmem_limit_bytes=40 * MIB),
        cost_estimate=pl.CostEstimate(
            flops=10 * HEADS * tokens * span * width,
            bytes_accessed=3 * MIB,
            transcendentals=HEADS * tokens * span,
        ),
    )(window, queries, d_out, bias, turned)


def query_kernel(ds_ref, kv_ref, dq_ref):
    tokens, width = kv_ref.shape[1], kv_ref.shape[2] // 2
    keys = kv_ref[:, :, :width].reshape(REACH * tokens, width)
    dq = jnp.dot(ds_ref[...], keys, preferred_element_type=jnp.float32).astype(jnp.bfloat16)
    for h in range(HEADS):
        dq_ref[:, h * width : (h + 1) * width] = dq[h * tokens : (h + 1) * tokens, :]


def query_grad(score_grad, window):
    tokens, width = window.shape[1], window.shape[2] // 2
    return pl.pallas_call(
        query_kernel,
        out_shape=jax.ShapeDtypeStruct((tokens, HEADS * width), jnp.bfloat16),
        in_specs=[VMEM] * 2,
        out_specs=VMEM,
        compiler_params=pltpu.CompilerParams(vmem_limit_bytes=16 * MIB),
        cost_estimate=pl.CostEstimate(
            flops=2 * HEADS * tokens * REACH * tokens * width, bytes_accessed=3 * MIB, transcendentals=0
        ),
    )(score_grad, window)


def gather_kernel(terms_ref, passed_ref, owned_ref):
    _, mine = position()
    passed = jnp.zeros(passed_ref.shape, jnp.float32)
    owned = jnp.zeros(owned_ref.shape, jnp.float32)
    for k, j in enumerate(ORDER):
        term = terms_ref[k].astype(jnp.float32)
        passed = passed + jnp.where(j < mine, term, 0.0)
        owned = owned + jnp.where(j < mine, 0.0, term)
    passed_ref[...] = passed.astype(jnp.bfloat16)
    owned_ref[...] = owned


def gather(terms):
    return pl.pallas_call(
        gather_kernel,
        out_shape=(pltpu.VMEM(terms.shape[1:], jnp.bfloat16), pltpu.VMEM(terms.shape[1:], jnp.float32)),
        in_specs=[VMEM],
        out_specs=(VMEM, VMEM),
        compiler_params=pltpu.CompilerParams(vmem_limit_bytes=16 * MIB),
    )(terms)


def body(queries, keys, values, d_out, doc_ids):
    n_inner = lax.axis_size("inner")
    total = lax.axis_size("outer") * n_inner
    tokens, width = keys.shape
    lines = [[start + j for j in ORDER] for start in range(0, n_inner, REACH)]

    def exchange(parts):
        return lax.all_to_all(parts, "inner", 0, 0, axis_index_groups=lines)

    packed = pack(keys, values)
    behind = lax.ppermute(packed, AXES, [(i, i + REACH) for i in range(total - REACH)])
    docs = doc_ids.reshape(-1, tokens)
    staged = prepare(queries, d_out, docs)
    behind, *staged = lax.optimization_barrier((behind, *staged))
    outgoing, bias, rows, grads, turned = route(packed, behind, queries, d_out, docs, staged)
    window = exchange(outgoing)
    attended, score_grad, parts = attention(window, rows, grads, bias, turned)
    passed, owned = gather(exchange(parts))
    passed = lax.ppermute(passed, AXES, [(i, i - REACH) for i in range(REACH, total)])
    grad_queries = query_grad(score_grad, window)
    owned = (owned + passed.astype(jnp.float32)).astype(jnp.bfloat16)
    return (attended, grad_queries, owned[:, :width], owned[:, width:])


def solution(mesh):
    split = P(("outer", "inner"), None)
    return jax.shard_map(
        body,
        mesh=mesh,
        in_specs=(split, split, split, split, P()),
        out_specs=(split, split, split, split),
        check_vma=False,
    )
```
